32 devices in a mesh: dp: 4 (over y, x), head: 8 (over z, core).
Axes of the slice: x: 2, y: 2, z: 4, core: 2. Of those that a mesh axis runs over, the one named last changes fastest.
Arguments:
- query: bfloat16 [4096, 12288], P(('dp', 'head')), may hold values from -160 to 160
- latent: bfloat16 [4096, 576], P(('dp', 'head')), may hold values from -6 to 6
- d_attn: bfloat16 [4096, 8192], P(('dp', 'head')), may hold values from -6 to 6
- w_kv: bfloat16 [512, 16384], P('dp', 'head'), may hold values from -0.25 to 0.25
- doc_lengths: int32 [4, 5], P('dp'), may hold values from 1 to 384, 1024 in all within a row
Outputs:
- d_query: bfloat16 [4096, 12288], P(('dp', 'head'))
- d_latent: float32 [4096, 576], P(('dp', 'head'))
- d_w_kv: float32 [512, 16384], P('dp', 'head')
The draws below stay inside these ranges and needn't reach their ends.
Inputs may be any that keep to these rules, and one draw needn't show every extreme that they name: `doc_lengths`: row g lists the lengths of the 5 documents of data group g; they sum to 1024, and the longest of each row is exactly 384.
All inputs are finite; a program needn't handle non-finite values.
Results may differ from the reference program's by a relative error of at most 0.025.
Values may be sent and summed in bfloat16 or wider, within the bound.
A program may use at most 128 MiB of HBM per device.

```python
import math
import jax
import jax.numpy as jnp
import numpy as np
from jax import lax

HEADS = 64
NOPE = 128
ROPE = 64
VDIM = 128
KV_RANK = 512
DOC_MAX = 384
QB = 128
SEQ = 1024
GROUPS = 4
TOKENS = 4096
NDOC = 5


def joint_tables(key):
    base = jax.random.fold_in(key, 4242)
    keys_list = jax.random.split(base, 2)
    latent = jnp.clip(jax.random.normal(keys_list[0], (TOKENS, KV_RANK + ROPE), jnp.float32), -6.0, 6.0)
    query = jnp.clip(jax.random.normal(keys_list[1], (TOKENS, HEADS * (NOPE + ROPE)), jnp.float32), -6.0, 6.0)
    return (query, latent)


def draw_query(key, part):
    return joint_tables(key)[0].astype(jnp.bfloat16)


def draw_latent(key, part):
    return joint_tables(key)[1].astype(jnp.bfloat16)


def steps_of(key, dims, pieces, low, top_value):
    level = 1.0
    for dim, shards_of in pieces:
        heights = jax.random.uniform(jax.random.fold_in(jax.random.fold_in(key, 6), dim), (shards_of,), jnp.float32, low / len(pieces), top_value / len(pieces))
        level = level * jnp.repeat(jnp.exp(heights), dims[dim] // shards_of).reshape((-1,) + (1,) * (len(dims) - 1 - dim))
    return level


def split_up(count, total, limit, skew):
    weights = [(1 << 20) // math.isqrt(standing ** skew) + 1 for standing in range(2, count + 1)]
    rest, holding = total - limit - (count - 1), [1] * (count - 1)
    while rest > 0:
        candidates = [i for i in range(count - 1) if holding[i] < limit]
        pool, budget = sum([weights[i] for i in candidates]), rest
        for i in candidates:
            addition = min(limit - holding[i], max(1, budget * weights[i] // pool), rest)
            holding[i] = holding[i] + addition
            rest = rest - addition
    return np.array([limit] + holding)


def ragged_sizes(stream_key, number_of, total, most, slope):
    if number_of == 2:
        one = jax.random.randint(stream_key, (), max(1, total - most), min(most, total - 1) + 1)
        return jnp.stack([one, total - one])
    sizes = jnp.asarray(split_up(number_of, total, most, slope), jnp.int32)
    couples = (number_of - 1) // 2
    source_of, sink = sizes[1:1 + 2 * couples:2], sizes[2:2 + 2 * couples:2]
    room = jnp.minimum(source_of - 1, most - sink)
    shifted = jax.random.randint(jax.random.fold_in(stream_key, 1), (couples,), 0, 1 << 20) % (room + 1)
    sizes = sizes.at[1:1 + 2 * couples:2].set(source_of - shifted).at[2:2 + 2 * couples:2].set(sink + shifted)
    return sizes[jax.random.permutation(jax.random.fold_in(stream_key, 2), number_of)]


def normal_values(key, extent, spread, limit, cuts=(), held_as=jnp.bfloat16):
    values = jax.random.normal(key, extent, jnp.float32) * spread
    if len(cuts) > 0:
        values = steps_of(key, extent, cuts, -0.22, 0.18) * values
    return jnp.clip(values, min=-limit, max=limit).astype(held_as)


def setup_inputs(seed: int = 0) -> dict:
    seeds = jax.random.split(jax.random.key(seed), 6)
    return {
        "query": draw_query(jax.random.fold_in(seeds[5], 71), 0),
        "latent": draw_latent(jax.random.fold_in(seeds[5], 71), 0),
        "d_attn": normal_values(seeds[2], (TOKENS, HEADS * VDIM), 1.0, 6.0, ((0, 32),)),
        "w_kv": normal_values(seeds[3], (KV_RANK, HEADS * (NOPE + VDIM)), KV_RANK ** -0.5, 0.25, ((0, 4), (1, 8))),
        "doc_lengths": jax.vmap(lambda own: ragged_sizes(own, NDOC, SEQ, DOC_MAX, 1))(jax.random.split(seeds[4], GROUPS)).reshape((GROUPS, NDOC)).astype(jnp.int32),
    }


masked_score = -1e+30

def document_index(lengths_row, count):
    ends = jnp.cumsum(lengths_row).astype(jnp.int32)
    positions = jnp.arange(count, dtype=jnp.int32)
    return lax.optimization_barrier(jnp.sum((positions[:, None] >= ends[None, :]).astype(jnp.int32), axis=1)).astype(jnp.int32)

def attend_backward(queries, keys_padded, values_padded, grads_out, doc_padded, block, window):
    seq_len = queries.shape[0]
    reach = window - block
    scale = 1.0 / math.sqrt(queries.shape[2])
    blocks = seq_len // block

    def one_block(carry, index):
        grad_keys, grad_values = carry
        first = index * block
        query_rows = lax.dynamic_slice_in_dim(queries, first, block, 0).astype(jnp.float32)
        key_rows = lax.dynamic_slice_in_dim(keys_padded, first, window, 0).astype(jnp.float32)
        value_rows = lax.dynamic_slice_in_dim(values_padded, first, window, 0).astype(jnp.float32)
        out_rows = lax.dynamic_slice_in_dim(grads_out, first, block, 0).astype(jnp.float32)
        query_doc = lax.dynamic_slice_in_dim(doc_padded, first + reach, block, 0)
        key_doc = lax.dynamic_slice_in_dim(doc_padded, first, window, 0)
        query_pos = jnp.arange(block, dtype=jnp.int32) + reach
        key_pos = jnp.arange(window, dtype=jnp.int32)
        allowed = (key_pos[None, :] <= query_pos[:, None]) & (key_doc[None, :] == query_doc[:, None])
        scores = jnp.einsum('qhd,khd->hqk', query_rows, key_rows) * scale
        scores = jnp.where(allowed[None], scores, masked_score)
        top = lax.optimization_barrier(jnp.max(scores, axis=2, keepdims=True))
        weights = jnp.exp(scores - top)
        probs = weights / lax.optimization_barrier(jnp.sum(weights, axis=2, keepdims=True))
        probs_low = probs.astype(jnp.bfloat16).astype(jnp.float32)
        attn_out = jnp.einsum('hqk,khd->qhd', probs_low, value_rows)
        delta = lax.optimization_barrier(jnp.sum(out_rows * attn_out, axis=2))
        dprob = jnp.einsum('qhd,khd->hqk', out_rows, value_rows)
        dscore = probs * (dprob - jnp.transpose(delta)[:, :, None])
        dscore_low = dscore.astype(jnp.bfloat16).astype(jnp.float32)
        grad_query = jnp.einsum('hqk,khd->qhd', dscore_low, key_rows) * scale
        grad_key_rows = jnp.einsum('hqk,qhd->khd', dscore_low, query_rows) * scale
        grad_value_rows = jnp.einsum('hqk,qhd->khd', probs_low, out_rows)
        grad_keys = lax.dynamic_update_slice_in_dim(grad_keys, lax.dynamic_slice_in_dim(grad_keys, first, window, 0) + grad_key_rows, first, 0)
        grad_values = lax.dynamic_update_slice_in_dim(grad_values, lax.dynamic_slice_in_dim(grad_values, first, window, 0) + grad_value_rows, first, 0)
        return ((grad_keys, grad_values), grad_query.astype(jnp.bfloat16))
    start_keys = jnp.zeros(keys_padded.shape, jnp.float32)
    start_values = jnp.zeros(values_padded.shape, jnp.float32)
    (grad_keys, grad_values), grad_queries = lax.scan(one_block, (start_keys, start_values), jnp.arange(blocks, dtype=jnp.int32))
    grad_queries = grad_queries.reshape(seq_len, queries.shape[1], queries.shape[2])
    return (grad_keys[reach:], grad_values[reach:], grad_queries)

def group_backward(query_g, latent_g, grads_g, w_kv, lengths_row):
    seq_len = query_g.shape[0]
    compressed = latent_g[:, :KV_RANK]
    kv_up = jnp.dot(compressed, w_kv, preferred_element_type=jnp.float32).astype(jnp.bfloat16)
    kv_up = kv_up.reshape(seq_len, HEADS, NOPE + VDIM)
    rotary = jnp.broadcast_to(latent_g[:, None, KV_RANK:], (seq_len, HEADS, ROPE))
    keys = jnp.concatenate([kv_up[:, :, :NOPE], rotary], axis=2)
    values = kv_up[:, :, NOPE:]
    keys_padded = jnp.concatenate([jnp.zeros((DOC_MAX, HEADS, NOPE + ROPE), keys.dtype), keys], axis=0)
    values_padded = jnp.concatenate([jnp.zeros((DOC_MAX, HEADS, VDIM), values.dtype), values], axis=0)
    doc_ids = document_index(lengths_row, seq_len)
    doc_padded = jnp.concatenate([jnp.full((DOC_MAX,), -1, jnp.int32), doc_ids]).astype(jnp.int32)
    grad_keys, grad_values, grad_queries = attend_backward(query_g.reshape(seq_len, HEADS, NOPE + ROPE), keys_padded, values_padded, grads_g.reshape(seq_len, HEADS, VDIM), doc_padded, QB, DOC_MAX + QB)
    grad_kv = jnp.concatenate([grad_keys[:, :, :NOPE], grad_values], axis=2).astype(jnp.bfloat16)
    grad_kv = grad_kv.reshape(seq_len, HEADS * (NOPE + VDIM))
    grad_weight = jnp.dot(jnp.transpose(compressed), grad_kv, preferred_element_type=jnp.float32)
    grad_compressed = jnp.dot(grad_kv, jnp.transpose(w_kv), preferred_element_type=jnp.float32)
    grad_rotary = lax.optimization_barrier(jnp.sum(grad_keys[:, :, NOPE:], axis=1))
    grad_latent = jnp.concatenate([grad_compressed, grad_rotary], axis=1)
    return (grad_queries.reshape(seq_len, HEADS * (NOPE + ROPE)), grad_latent, grad_weight)

def reference(query, latent, d_attn, w_kv, doc_lengths):

    def one_group(carry, index):
        first = index * SEQ
        query_g = lax.dynamic_slice_in_dim(query, first, SEQ, 0)
        latent_g = lax.dynamic_slice_in_dim(latent, first, SEQ, 0)
        grads_g = lax.dynamic_slice_in_dim(d_attn, first, SEQ, 0)
        lengths_row = lax.dynamic_index_in_dim(doc_lengths, index, 0, keepdims=False)
        grad_q, grad_l, grad_w = group_backward(query_g, latent_g, grads_g, w_kv, lengths_row)
        return (carry + grad_w, (grad_q, grad_l))
    start_weight = jnp.zeros((KV_RANK, HEADS * (NOPE + VDIM)), jnp.float32)
    total_weight, (all_q, all_l) = lax.scan(one_group, start_weight, jnp.arange(GROUPS, dtype=jnp.int32))
    d_query = all_q.reshape(TOKENS, HEADS * (NOPE + ROPE))
    d_latent = all_l.reshape(TOKENS, KV_RANK + ROPE)
    return (d_query, d_latent, total_weight)
```

```python
import functools
import math

import jax
import jax.numpy as jnp
from jax import lax
from jax.experimental import pallas as pl
from jax.experimental.pallas import tpu as pltpu
from jax.sharding import PartitionSpec as P

NOPE = 128
ROPE = 64
VDIM = 128
KV_RANK = 512
DOC_MAX = 384
QB = 128
MEMBERS = 4
MESH = pl.DeviceIdType.MESH

masked_score = -1e30
NN = (((1,), (0,)), ((), ()))
NT = (((1,), (1,)), ((), ()))
TN = (((0,), (0,)), ((), ()))


def dot(a, b, dims):
    return lax.dot_general(a, b, dims, preferred_element_type=jnp.float32)


def kernel(
    cfg,
    query,
    d_attn,
    latent,
    latent_t,
    w,
    starts,
    d_query,
    d_w,
    d_lat,
    q_buf,
    o_buf,
    dq_buf,
    keys,
    vals,
    dk_acc,
    dv_acc,
    dkv,
    dlat_acc,
    rope_acc,
    q_send,
    q_recv,
    o_send,
    o_recv,
    dq_send,
    dq_recv,
):
    members, parts, pairs, own = cfg
    chunks = parts * pairs
    dp = lax.axis_index("dp")
    head = lax.axis_index("head")
    part = head // members
    me = lax.rem(head, members)
    window = latent.shape[0]
    reach = window - members * own
    qw = 2 * (NOPE + ROPE)
    ow = 2 * VDIM
    scale = 1.0 / math.sqrt(NOPE + ROPE)
    to_exp2 = scale * math.log2(math.e)

    def other(k):
        return lax.rem(me + k, members)

    def place(c):
        return lax.rem(part + c // pairs, parts), lax.rem(c, pairs)

    def pair_index(member, c):
        p, j = place(c)
        return (member + members * p) * pairs + j

    barrier = pltpu.get_barrier_semaphore()
    for k in range(1, members):
        pl.semaphore_signal(
            barrier, inc=1, device_id=(dp, part * members + other(k)), device_id_type=MESH
        )
    pl.semaphore_wait(barrier, members - 1)

    def move(src, dst, send, recv, c, k):
        if k == 0:
            return pltpu.make_async_copy(src, dst, send.at[c, 0])
        return pltpu.make_async_remote_copy(
            src_ref=src,
            dst_ref=dst,
            send_sem=send.at[c, k],
            recv_sem=recv.at[c, k],
            device_id=(dp, part * members + other(k)),
            device_id_type=MESH,
        )

    def q_copy(c, k):
        col = pl.multiple_of(pair_index(other(k), c) * qw, 128)
        row = pl.multiple_of(me * own, own)
        return move(
            query.at[:, pl.ds(col, qw)], q_buf.at[c, pl.ds(row, own)], q_send, q_recv, c, k
        )

    def o_copy(c, k):
        col = pl.multiple_of(pair_index(other(k), c) * ow, 128)
        row = pl.multiple_of(me * own, own)
        return move(
            d_attn.at[:, pl.ds(col, ow)], o_buf.at[c, pl.ds(row, own)], o_send, o_recv, c, k
        )

    def dq_copy(c, k):
        col = pl.multiple_of(pair_index(me, c) * qw, 128)
        row = pl.multiple_of(other(k) * own, own)
        return move(
            dq_buf.at[c, pl.ds(row, own)], d_query.at[:, pl.ds(col, qw)], dq_send, dq_recv, c, k
        )

    @pl.loop(0, chunks)
    def _(c):
        for k in list(range(1, members)) + [0]:
            q_copy(c, k).start()
            o_copy(c, k).start()

    dlat_acc[...] = jnp.zeros_like(dlat_acc)
    rope_acc[...] = jnp.zeros_like(rope_acc)
    rope = latent[:, KV_RANK:].astype(jnp.float32)
    empty = jnp.zeros_like(rope)
    half = NOPE // 2
    keys[0, :, NOPE:] = jnp.concatenate([rope, empty], axis=1).astype(jnp.bfloat16)
    keys[2] = jnp.concatenate([empty, rope, empty, rope], axis=1).astype(jnp.bfloat16)
    lane = lax.broadcasted_iota(jnp.int32, (window, NOPE), 1)

    @pl.loop(0, chunks)
    def _(c):
        p, j = place(c)
        cols = pl.ds(pl.multiple_of(j * 512, 512), 2 * (NOPE + VDIM))
        kv = dot(latent[:, :KV_RANK], w[p, :, cols], NN)
        keys[0, :, :NOPE] = kv[:, :NOPE].astype(jnp.bfloat16)
        vals[0] = kv[:, NOPE : 2 * NOPE].astype(jnp.bfloat16)
        rolled = pltpu.roll(kv[:, 2 * NOPE : 3 * NOPE], half, 1)
        keys[1, :, :NOPE] = jnp.where(lane < half, 0.0, rolled).astype(jnp.bfloat16)
        keys[1, :, NOPE:] = jnp.where(
            lane < half, rolled.astype(jnp.bfloat16).astype(jnp.float32),
            keys[2, :, NOPE:].astype(jnp.float32),
        ).astype(jnp.bfloat16)
        vals[1] = kv[:, 3 * NOPE :].astype(jnp.bfloat16)
        for k in range(members):
            if k == 0:
                q_copy(c, k).wait()
                o_copy(c, k).wait()
            else:
                q_copy(c, k).wait_recv()
                o_copy(c, k).wait_recv()
        dk_acc[...] = jnp.zeros_like(dk_acc)
        dv_acc[...] = jnp.zeros_like(dv_acc)
        for b in range(members * own // QB):
            rows = slice(b * QB, (b + 1) * QB)
            span = slice(b * QB, b * QB + reach + QB)
            shape = (reach + QB, QB)
            key_pos = lax.broadcasted_iota(jnp.int32, shape, 0) + b * QB
            query_pos = lax.broadcasted_iota(jnp.int32, shape, 1) + (reach + b * QB)
            allowed = (key_pos <= query_pos) & (key_pos >= starts[:, rows])
            grads = []
            for h in range(2):
                q = q_buf[c, rows, h * NOPE : h * NOPE + 2 * NOPE]
                o = o_buf[c, rows, h * VDIM : (h + 1) * VDIM]
                key = keys[h, span]
                s = dot(key, q, NT)
                s = jnp.where(allowed, s, masked_score)
                top = jnp.max(s, axis=0, keepdims=True)
                e = jnp.exp2((s - top) * to_exp2)
                probs = e * (1.0 / jnp.sum(e, axis=0, keepdims=True))
                low = probs.astype(jnp.bfloat16)
                dprob = dot(vals[h, span], o, NT)
                delta = jnp.sum(low.astype(jnp.float32) * dprob, axis=0, keepdims=True)
                ds = (probs * (dprob - delta)).astype(jnp.bfloat16)
                dv_acc[h, span] += dot(low, o, NN)
                dk_acc[h, span] += dot(ds, q, NN)
                grads.append(dot(ds, key, TN) * scale)
            a, z = grads
            dq_buf[c, rows, :NOPE] = a[:, :NOPE].astype(jnp.bfloat16)
            dq_buf[c, rows, NOPE : 2 * NOPE] = (a[:, NOPE:] + z[:, :NOPE]).astype(jnp.bfloat16)
            dq_buf[c, rows, 2 * NOPE :] = z[:, NOPE:].astype(jnp.bfloat16)
        for k in list(range(1, members)) + [0]:
            dq_copy(c, k).start()
        low_lane = lane < half
        dkv[:, :NOPE] = (dk_acc[0, :, :NOPE] * scale).astype(jnp.bfloat16)
        dkv[:, NOPE : 2 * NOPE] = dv_acc[0].astype(jnp.bfloat16)
        turned_a = pltpu.roll(dk_acc[1, :, :NOPE], half, 1)
        turned_b = pltpu.roll(dk_acc[1, :, NOPE:], half, 1)
        dkv[:, 2 * NOPE : 3 * NOPE] = (
            jnp.where(low_lane, turned_a, turned_b) * scale
        ).astype(jnp.bfloat16)
        dkv[:, 3 * NOPE :] = dv_acc[1].astype(jnp.bfloat16)
        rope_acc[...] += dk_acc[0, :, NOPE:] + turned_b
        dlat_acc[...] += dot(dkv[...], w[p, :, cols], NT)
        d_w[p, :, cols] = dot(latent_t[...], dkv[...], NN).astype(jnp.bfloat16)

    d_lat[:, :KV_RANK] = dlat_acc[...]
    d_lat[:, KV_RANK:] = rope_acc[:, :ROPE] * scale

    @pl.loop(0, chunks)
    def _(c):
        for k in range(members):
            if k == 0:
                dq_copy(c, k).wait()
            else:
                q_copy(c, k).wait_send()
                o_copy(c, k).wait_send()
                dq_copy(c, k).wait()


def local(query, latent, d_attn, w_kv, doc_lengths):
    group = lax.axis_size("head")
    head = lax.axis_index("head")
    own = query.shape[0]
    members = min(MEMBERS, group)
    parts = group // members
    seq = own * group
    held = members * own
    pairs = w_kv.shape[1] // (2 * (NOPE + VDIM))
    chunks = parts * pairs
    window = DOC_MAX + held
    first = (head // members) * held
    across = [[m + members * p for p in range(parts)] for m in range(members)]

    latents = lax.all_gather(latent, "head", axis=0, tiled=True)
    padded = jnp.concatenate([jnp.zeros((DOC_MAX, latent.shape[1]), latent.dtype), latents], axis=0)
    near = lax.dynamic_slice_in_dim(padded, first, window, 0)
    both = lax.all_gather(w_kv, "head", axis=0, axis_index_groups=across)
    weight = lax.all_gather(both, "dp", axis=1, tiled=True)

    ends = jnp.cumsum(doc_lengths[0])
    positions = first + jnp.arange(held, dtype=jnp.int32)
    starts = jnp.max(jnp.where(ends[None, :] <= positions[:, None], ends[None, :], 0), axis=1)
    starts = (starts - first + DOC_MAX).astype(jnp.int32)[None, :]

    hbm = pl.BlockSpec(memory_space=pl.ANY)
    vmem = pl.BlockSpec(memory_space=pltpu.VMEM)
    bf16, f32 = jnp.bfloat16, jnp.float32
    qw, ow, cw = 2 * (NOPE + ROPE), 2 * VDIM, 2 * (NOPE + VDIM)
    sems = [pltpu.SemaphoreType.DMA((chunks, members))] * 6
    d_query, d_w, d_lat = pl.pallas_call(
        functools.partial(kernel, (members, parts, pairs, own)),
        out_shape=(
            jax.ShapeDtypeStruct(query.shape, bf16),
            jax.ShapeDtypeStruct(weight.shape, bf16),
            jax.ShapeDtypeStruct(near.shape, f32),
        ),
        in_specs=[hbm, hbm, vmem, vmem, vmem, vmem],
        out_specs=(hbm, vmem, vmem),
        scratch_shapes=[
            pltpu.VMEM((chunks, held, qw), bf16),
            pltpu.VMEM((chunks, held, ow), bf16),
            pltpu.VMEM((chunks, held, qw), bf16),
            pltpu.VMEM((3, window, 2 * NOPE), bf16),
            pltpu.VMEM((2, window, VDIM), bf16),
            pltpu.VMEM((2, window, 2 * NOPE), f32),
            pltpu.VMEM((2, window, VDIM), f32),
            pltpu.VMEM((window, cw), bf16),
            pltpu.VMEM((window, KV_RANK), f32),
            pltpu.VMEM((window, NOPE), f32),
        ]
        + sems,
        compiler_params=pltpu.CompilerParams(
            collective_id=0, has_side_effects=True, vmem_limit_bytes=56 * 2**20
        ),
    )(query, d_attn, near, jnp.transpose(near[:, :KV_RANK]), weight, starts)

    grad_w = lax.psum_scatter(d_w, "dp", scatter_dimension=1, tiled=True)
    grad_w = lax.psum_scatter(grad_w, "head", scatter_dimension=0, axis_index_groups=across)
    whole = lax.dynamic_update_slice_in_dim(
        jnp.zeros((DOC_MAX + seq, near.shape[1]), bf16), d_lat.astype(bf16), first, 0
    )
    grad_latent = lax.psum_scatter(whole[DOC_MAX:], "head", scatter_dimension=0, tiled=True)
    return (d_query, grad_latent.astype(f32), grad_w.astype(f32))


def solution(mesh):
    placed = (
        P(("dp", "head"), None),
        P(("dp", "head"), None),
        P(("dp", "head"), None),
        P("dp", "head"),
        P("dp", None),
    )
    return jax.shard_map(
        local,
        mesh=mesh,
        in_specs=placed,
        out_specs=(P(("dp", "head"), None), P(("dp", "head"), None), P("dp", "head")),
        check_vma=False,
    )
```

```python
import functools
import math

import jax
import jax.numpy as jnp
from jax import lax
from jax.experimental import pallas as pl
from jax.experimental.pallas import tpu as pltpu
from jax.sharding import PartitionSpec as P

NOPE = 128
ROPE = 64
VDIM = 128
KV_RANK = 512
DOC_MAX = 384
QB = 128
MEMBERS = 4
AHEAD = 3
LAG = 2
MESH = pl.DeviceIdType.MESH

masked_score = -1e30
NN = (((1,), (0,)), ((), ()))
NT = (((1,), (1,)), ((), ()))
TN = (((0,), (0,)), ((), ()))


def dot(a, b, dims):
    return lax.dot_general(a, b, dims, preferred_element_type=jnp.float32)


def kernel(
    cfg,
    query,
    d_attn,
    latent,
    w_kv,
    starts,
    d_query,
    d_latent,
    d_w,
    q_buf,
    o_buf,
    dq_buf,
    w_buf,
    lat_buf,
    lat_t,
    keys,
    vals,
    dk_acc,
    dv_acc,
    dkv,
    dlat_acc,
    rope_acc,
    dw_part,
    dw_got,
    dw_mid,
    dw_fin,
    dl_part,
    dl_got,
    dl_mid,
    dl_fin,
    q_send,
    q_recv,
    o_send,
    o_recv,
    dq_send,
    dq_recv,
    w_send,
    w_recv,
    px_send,
    px_recv,
    dw_send,
    dw_recv,
    dz_send,
    dz_recv,
    lat_send,
    lat_recv,
    dl_send,
    dl_recv,
    one_send,
    one_recv,
):
    members, parts, pairs, groups = cfg
    chunks = parts * pairs
    dp = lax.axis_index("dp")
    head = lax.axis_index("head")
    part = head // members
    me = lax.rem(head, members)
    own = query.shape[0]
    held = members * own
    pad = held - DOC_MAX
    window = DOC_MAX + held
    depth = w_kv.shape[0]
    qw = 2 * (NOPE + ROPE)
    ow = 2 * VDIM
    cw = 2 * (NOPE + VDIM)
    scale = 1.0 / math.sqrt(NOPE + ROPE)
    to_exp2 = scale * math.log2(math.e)
    f32, bf16 = jnp.float32, jnp.bfloat16

    def other(k):
        return lax.rem(me + k, members)

    def peer(k):
        return (dp, part * members + other(k))

    def across(r):
        return (dp, lax.rem(part + r, parts) * members + me)

    def beside(k):
        return (lax.rem(dp + k, groups), head)

    def rows_of(index, count):
        return pl.ds(pl.multiple_of(index * count, count), count)

    def place(c):
        return lax.rem(part + c // pairs, parts), lax.rem(c, pairs)

    def pair_index(member, c):
        p, j = place(c)
        return (member + members * p) * pairs + j

    def remote(src, dst, send, recv, device):
        return pltpu.make_async_remote_copy(
            src_ref=src,
            dst_ref=dst,
            send_sem=send,
            recv_sem=recv,
            device_id=device,
            device_id_type=MESH,
        )

    def move(src, dst, send, recv, c, k):
        if k == 0:
            return pltpu.make_async_copy(src, dst, send.at[c, 0])
        return remote(src, dst, send.at[c, k], recv.at[c, k], peer(k))

    def q_copy(c, k):
        col = pl.multiple_of(pair_index(other(k), c) * qw, 128)
        dst = q_buf.at[c, rows_of(me, own)]
        return move(query.at[:, pl.ds(col, qw)], dst, q_send, q_recv, c, k)

    def o_copy(c, k):
        col = pl.multiple_of(pair_index(other(k), c) * ow, 128)
        dst = o_buf.at[c, rows_of(me, own)]
        return move(d_attn.at[:, pl.ds(col, ow)], dst, o_send, o_recv, c, k)

    def dq_copy(c, k):
        col = pl.multiple_of(pair_index(me, c) * qw, 128)
        src = dq_buf.at[c, rows_of(other(k), own)]
        return move(src, d_query.at[:, pl.ds(col, qw)], dq_send, dq_recv, c, k)

    def w_columns(c):
        return pl.ds(pl.multiple_of(lax.rem(c, pairs) * cw, cw), cw)

    def w_own(c):
        dst = w_buf.at[c, rows_of(dp, depth)]
        return pltpu.make_async_copy(w_kv.at[:, w_columns(c)], dst, px_send.at[c])

    def w_cross(c):
        dst = w_buf.at[c, rows_of(dp, depth)]
        device = across(parts - c // pairs)
        return remote(w_kv.at[:, w_columns(c)], dst, px_send.at[c], px_recv.at[c], device)

    def w_copy(c, k):
        block = w_buf.at[c, rows_of(dp, depth)]
        return remote(block, block, w_send.at[c, k], w_recv.at[c, k], beside(k))

    def dw_copy(c, k):
        src = dw_part.at[c, rows_of(lax.rem(dp + k, groups), depth)]
        return remote(src, dw_got.at[c, k], dw_send.at[c, k], dw_recv.at[c, k], beside(k))

    def dz_copy(c):
        device = across(c // pairs)
        return remote(dw_mid.at[c], dw_fin.at[c], dz_send.at[c], dz_recv.at[c], device)

    def lat_copy(side, k):
        block = lat_buf.at[side, rows_of(me, own)]
        if k == 0:
            return pltpu.make_async_copy(latent, block, lat_send.at[side, 0])
        src = latent if side == 1 else block
        return remote(src, block, lat_send.at[side, k], lat_recv.at[side, k], peer(k))

    def lat_cross():
        dst = lat_buf.at[0, rows_of(me, own)]
        return remote(latent, dst, one_send.at[0], one_recv.at[0], across(1))

    def dl_copy(k):
        src = dl_part.at[other(k)]
        return remote(src, dl_got.at[k], dl_send.at[k], dl_recv.at[k], peer(k))

    def dl_cross():
        return remote(dl_mid, dl_fin, one_send.at[1], one_recv.at[1], across(parts - 1))

    def launch(c):
        for k in list(range(1, members)) + [0]:
            q_copy(c, k).start()
            o_copy(c, k).start()

        @pl.when(c < pairs)
        def _():
            w_own(c).wait()

        @pl.when(c >= pairs)
        def _():
            w_cross(c).wait_recv()

        @pl.loop(1, groups)
        def _(k):
            w_copy(c, k).start()

    barrier = pltpu.get_barrier_semaphore()

    def greet(device):
        pl.semaphore_signal(barrier, inc=1, device_id=device, device_id_type=MESH)

    for k in range(1, members):
        greet(peer(k))
    for r in range(1, parts):
        greet(across(r))

    @pl.loop(1, groups)
    def _(k):
        greet(beside(k))

    pl.semaphore_wait(barrier, members + parts + groups - 3)

    lat_cross().start()
    for k in list(range(1, members)) + [0]:
        lat_copy(1, k).start()

    @pl.loop(0, pairs)
    def _(c):
        w_own(c).start()

    @pl.loop(pairs, chunks)
    def _(c):
        w_cross(c).start()

    launch(jnp.int32(0))
    lat_cross().wait_recv()
    for k in range(1, members):
        lat_copy(0, k).start()

    @pl.loop(1, AHEAD)
    def _(c):
        launch(c)

    dlat_acc[...] = jnp.zeros_like(dlat_acc)
    rope_acc[...] = jnp.zeros_like(rope_acc)
    lat_copy(1, 0).wait()
    for k in range(1, members):
        lat_copy(1, k).wait_recv()
        lat_copy(0, k).wait_recv()

    half = NOPE // 2
    lane = lax.broadcasted_iota(jnp.int32, (window, NOPE), 1)
    low_lane = lane < half
    near = jnp.concatenate([lat_buf[0, pad:], lat_buf[1]], axis=0)
    lat_t[...] = jnp.transpose(near[:, :KV_RANK])
    rope = near[:, KV_RANK:].astype(f32)
    empty = jnp.zeros_like(rope)
    keys[0, :, NOPE:] = jnp.concatenate([rope, empty], axis=1).astype(bf16)
    keys[2, :, NOPE:] = jnp.concatenate([empty, rope], axis=1).astype(bf16)

    def settle(c):
        @pl.loop(1, groups)
        def _(k):
            dw_copy(c, k).wait_recv()

        total = dw_part[c, rows_of(dp, depth)].astype(f32)
        for k in range(1, groups):
            total += dw_got[c, k].astype(f32)

        @pl.when(c < pairs)
        def _():
            d_w[:, w_columns(c)] = total

        @pl.when(c >= pairs)
        def _():
            dw_mid[c] = total.astype(bf16)
            dz_copy(c).start()

    @pl.loop(0, chunks)
    def _(c):
        @pl.when(c + AHEAD < chunks)
        def _():
            launch(c + AHEAD)

        @pl.when(c >= LAG)
        def _():
            settle(c - LAG)

        @pl.loop(1, groups)
        def _(k):
            w_copy(c, k).wait_recv()

        weight = w_buf.at[c]
        split = DOC_MAX
        for side, rows in ((0, slice(0, split)), (1, slice(split, window))):
            lat = lat_buf[0, pad:, :KV_RANK] if side == 0 else lat_buf[1, :, :KV_RANK]
            kv = dot(lat, weight[...], NN)
            keys[0, rows, :NOPE] = kv[:, :NOPE].astype(bf16)
            vals[0, rows] = kv[:, NOPE : 2 * NOPE].astype(bf16)
            rolled = pltpu.roll(kv[:, 2 * NOPE : 3 * NOPE], half, 1)
            lower = low_lane[rows]
            keys[1, rows, :NOPE] = jnp.where(lower, 0.0, rolled).astype(bf16)
            keys[1, rows, NOPE:] = jnp.where(
                lower, rolled, keys[2, rows, NOPE:].astype(f32)
            ).astype(bf16)
            vals[1, rows] = kv[:, 3 * NOPE :].astype(bf16)
        for k in range(members):
            if k == 0:
                q_copy(c, k).wait()
                o_copy(c, k).wait()
            else:
                q_copy(c, k).wait_recv()
                o_copy(c, k).wait_recv()
        dk_acc[...] = jnp.zeros_like(dk_acc)
        dv_acc[...] = jnp.zeros_like(dv_acc)
        for b in range(held // QB):
            rows = slice(b * QB, (b + 1) * QB)
            span = slice(b * QB, b * QB + DOC_MAX + QB)
            shape = (DOC_MAX + QB, QB)
            key_pos = lax.broadcasted_iota(jnp.int32, shape, 0) + b * QB
            query_pos = lax.broadcasted_iota(jnp.int32, shape, 1) + (DOC_MAX + b * QB)
            allowed = (key_pos <= query_pos) & (key_pos >= starts[:, rows])
            grads = []
            for h in range(2):
                q = q_buf[c, rows, h * NOPE : h * NOPE + 2 * NOPE]
                o = o_buf[c, rows, h * VDIM : (h + 1) * VDIM]
                key = keys[h, span]
                s = dot(key, q, NT)
                s = jnp.where(allowed, s, masked_score)
                top = jnp.max(s, axis=0, keepdims=True)
                e = jnp.exp2((s - top) * to_exp2)
                probs = e * (1.0 / jnp.sum(e, axis=0, keepdims=True))
                low = probs.astype(bf16)
                dprob = dot(vals[h, span], o, NT)
                delta = jnp.sum(low.astype(f32) * dprob, axis=0, keepdims=True)
                ds = (probs * (dprob - delta)).astype(bf16)
                dv_acc[h, span] += dot(low, o, NN)
                dk_acc[h, span] += dot(ds, q, NN)
                grads.append(dot(ds, key, TN) * scale)
            a, z = grads
            dq_buf[c, rows, :NOPE] = a[:, :NOPE].astype(bf16)
            dq_buf[c, rows, NOPE : 2 * NOPE] = (a[:, NOPE:] + z[:, :NOPE]).astype(bf16)
            dq_buf[c, rows, 2 * NOPE :] = z[:, NOPE:].astype(bf16)
        for k in list(range(1, members)) + [0]:
            dq_copy(c, k).start()
        dkv[:, :NOPE] = (dk_acc[0, :, :NOPE] * scale).astype(bf16)
        dkv[:, NOPE : 2 * NOPE] = dv_acc[0].astype(bf16)
        turned_a = pltpu.roll(dk_acc[1, :, :NOPE], half, 1)
        turned_b = pltpu.roll(dk_acc[1, :, NOPE:], half, 1)
        dkv[:, 2 * NOPE : 3 * NOPE] = (jnp.where(low_lane, turned_a, turned_b) * scale).astype(bf16)
        dkv[:, 3 * NOPE :] = dv_acc[1].astype(bf16)
        dw_part[c] = dot(lat_t[...], dkv[...], NN).astype(bf16)

        @pl.loop(1, groups)
        def _(k):
            dw_copy(c, k).start()

        rope_acc[...] += dk_acc[0, :, NOPE:] + turned_b
        dlat_acc[...] += dot(dkv[...], weight[...], NT)

    for index in range(2 * members):
        side, m, first = index // members, index % members, index * own - pad
        if first < 0:
            dl_part[m, side] = jnp.zeros_like(dl_part[m, side])
        else:
            rows = slice(first, first + own)
            dl_part[m, side, :, :KV_RANK] = dlat_acc[rows].astype(bf16)
            dl_part[m, side, :, KV_RANK:] = (rope_acc[rows, :ROPE] * scale).astype(bf16)
    for k in range(1, members):
        dl_copy(k).start()

    @pl.loop(chunks - LAG, chunks)
    def _(c):
        settle(c)

    for k in range(1, members):
        dl_copy(k).wait_recv()
    back = dl_part[me, 0].astype(f32)
    kept = dl_part[me, 1].astype(f32)
    for k in range(1, members):
        back += dl_got[k, 0].astype(f32)
        kept += dl_got[k, 1].astype(f32)
    dl_mid[...] = back.astype(bf16)
    dl_cross().start()

    @pl.loop(pairs, chunks)
    def _(c):
        dz_copy(c).wait()
        d_w[:, w_columns(c)] += dw_fin[c].astype(f32)

    dl_cross().wait()
    d_latent[...] = kept + dl_fin[...].astype(f32)

    lat_cross().wait_send()
    for k in range(1, members):
        lat_copy(0, k).wait_send()
        lat_copy(1, k).wait_send()
        dl_copy(k).wait_send()

    @pl.loop(pairs, chunks)
    def _(c):
        w_cross(c).wait_send()

    @pl.loop(0, chunks)
    def _(c):
        for k in range(members):
            if k == 0:
                dq_copy(c, k).wait()
            else:
                q_copy(c, k).wait_send()
                o_copy(c, k).wait_send()
                dq_copy(c, k).wait()

        @pl.loop(1, groups)
        def _(k):
            w_copy(c, k).wait_send()
            dw_copy(c, k).wait_send()


def local(query, latent, d_attn, w_kv, doc_lengths):
    group = lax.axis_size("head")
    groups = lax.axis_size("dp")
    head = lax.axis_index("head")
    own, wide = latent.shape
    members = min(MEMBERS, group // 2)
    parts = group // members
    held = members * own
    depth = w_kv.shape[0]
    pairs = w_kv.shape[1] // (2 * (NOPE + VDIM))
    chunks = parts * pairs
    window = DOC_MAX + held
    first = (head // members) * held

    ends = jnp.cumsum(doc_lengths[0])
    positions = first + jnp.arange(held, dtype=jnp.int32)
    starts = jnp.max(jnp.where(ends[None, :] <= positions[:, None], ends[None, :], 0), axis=1)
    starts = (starts - first + DOC_MAX).astype(jnp.int32)[None, :]

    hbm = pl.BlockSpec(memory_space=pl.ANY)
    vmem = pl.BlockSpec(memory_space=pltpu.VMEM)
    bf16, f32 = jnp.bfloat16, jnp.float32
    qw, ow, cw = 2 * (NOPE + ROPE), 2 * VDIM, 2 * (NOPE + VDIM)
    by_member = pltpu.SemaphoreType.DMA((chunks, members))
    by_group = pltpu.SemaphoreType.DMA((chunks, groups))
    by_chunk = pltpu.SemaphoreType.DMA((chunks,))
    few = pltpu.SemaphoreType.DMA((2, members))
    return pl.pallas_call(
        functools.partial(kernel, (members, parts, pairs, groups)),
        out_shape=(
            jax.ShapeDtypeStruct(query.shape, bf16),
            jax.ShapeDtypeStruct(latent.shape, f32),
            jax.ShapeDtypeStruct(w_kv.shape, f32),
        ),
        in_specs=[hbm, hbm, hbm, hbm, vmem],
        out_specs=(hbm, vmem, vmem),
        scratch_shapes=[
            pltpu.VMEM((chunks, held, qw), bf16),
            pltpu.VMEM((chunks, held, ow), bf16),
            pltpu.VMEM((chunks, held, qw), bf16),
            pltpu.VMEM((chunks, KV_RANK, cw), bf16),
            pltpu.VMEM((2, held, wide), bf16),
            pltpu.VMEM((KV_RANK, window), bf16),
            pltpu.VMEM((3, window, 2 * NOPE), bf16),
            pltpu.VMEM((2, window, VDIM), bf16),
            pltpu.VMEM((2, window, 2 * NOPE), f32),
            pltpu.VMEM((2, window, VDIM), f32),
            pltpu.VMEM((window, cw), bf16),
            pltpu.VMEM((window, KV_RANK), f32),
            pltpu.VMEM((window, NOPE), f32),
            pltpu.VMEM((chunks, KV_RANK, cw), bf16),
            pltpu.VMEM((chunks, groups, depth, cw), bf16),
            pltpu.VMEM((chunks, depth, cw), bf16),
            pltpu.VMEM((chunks, depth, cw), bf16),
            pltpu.VMEM((members, 2, own, wide), bf16),
            pltpu.VMEM((members, 2, own, wide), bf16),
            pltpu.VMEM((own, wide), bf16),
            pltpu.VMEM((own, wide), bf16),
        ]
        + [by_member] * 6
        + [by_group] * 2
        + [by_chunk] * 2
        + [by_group] * 2
        + [by_chunk] * 2
        + [few] * 2
        + [pltpu.SemaphoreType.DMA((members,))] * 2
        + [pltpu.SemaphoreType.DMA((2,))] * 2,
        compiler_params=pltpu.CompilerParams(
            collective_id=0, has_side_effects=True, vmem_limit_bytes=56 * 2**20
        ),
    )(query, d_attn, latent, w_kv, starts)


def solution(mesh):
    placed = (
        P(("dp", "head"), None),
        P(("dp", "head"), None),
        P(("dp", "head"), None),
        P("dp", "head"),
        P("dp", None),
    )
    return jax.shard_map(
        local,
        mesh=mesh,
        in_specs=placed,
        out_specs=(P(("dp", "head"), None), P(("dp", "head"), None), P("dp", "head")),
        check_vma=False,
    )
```

```python
import functools
import math

import jax
import jax.numpy as jnp
from jax import lax
from jax.experimental import pallas as pl
from jax.experimental.pallas import tpu as pltpu
from jax.sharding import PartitionSpec as P

NOPE = 128
ROPE = 64
VDIM = 128
KV_RANK = 512
DOC_MAX = 384
QB = 256
MEMBERS = 4
AHEAD = 3
LAG = 2
MESH = pl.DeviceIdType.MESH

masked_score = -1e30
NN = (((1,), (0,)), ((), ()))
NT = (((1,), (1,)), ((), ()))
TN = (((0,), (0,)), ((), ()))


def dot(a, b, dims):
    return lax.dot_general(a, b, dims, preferred_element_type=jnp.float32)


def kernel(
    cfg,
    query,
    d_attn,
    latent,
    w_kv,
    starts,
    d_query,
    d_latent,
    d_w,
    q_buf,
    o_buf,
    dq_buf,
    w_buf,
    lat_buf,
    lat_t,
    keys,
    vals,
    dk_acc,
    dv_acc,
    dkv,
    dlat_acc,
    rope_acc,
    dw_part,
    dw_got,
    dw_mid,
    dw_fin,
    dl_part,
    dl_sum,
    dl_got,
    dl_mid,
    dl_fin,
    q_send,
    q_recv,
    o_send,
    o_recv,
    dq_send,
    dq_recv,
    w_send,
    w_recv,
    px_send,
    px_recv,
    dw_send,
    dw_recv,
    dz_send,
    dz_recv,
    lat_send,
    lat_recv,
    dl_send,
    dl_recv,
    one_send,
    one_recv,
):
    members, parts, pairs, groups = cfg
    chunks = parts * pairs
    dp = lax.axis_index("dp")
    head = lax.axis_index("head")
    part = head // members
    me = lax.rem(head, members)
    own = query.shape[0]
    held = members * own
    pad = held - DOC_MAX
    window = DOC_MAX + held
    depth = w_kv.shape[0]
    qw = 2 * (NOPE + ROPE)
    ow = 2 * VDIM
    cw = 2 * (NOPE + VDIM)
    scale = 1.0 / math.sqrt(NOPE + ROPE)
    to_exp2 = scale * math.log2(math.e)
    f32, bf16 = jnp.float32, jnp.bfloat16

    def other(k):
        return lax.rem(me + k, members)

    def peer(k):
        return (dp, part * members + other(k))

    def across(r):
        return (dp, lax.rem(part + r, parts) * members + me)

    def beside(k):
        return (lax.rem(dp + k, groups), head)

    def rows_of(index, count):
        return pl.ds(pl.multiple_of(index * count, count), count)

    def place(c):
        return lax.rem(part + c // pairs, parts), lax.rem(c, pairs)

    def pair_index(member, c):
        p, j = place(c)
        return (member + members * p) * pairs + j

    def remote(src, dst, send, recv, device):
        return pltpu.make_async_remote_copy(
            src_ref=src,
            dst_ref=dst,
            send_sem=send,
            recv_sem=recv,
            device_id=device,
            device_id_type=MESH,
        )

    def move(src, dst, send, recv, c, k):
        if k == 0:
            return pltpu.make_async_copy(src, dst, send.at[c, 0])
        return remote(src, dst, send.at[c, k], recv.at[c, k], peer(k))

    def q_copy(c, k):
        col = pl.multiple_of(pair_index(other(k), c) * qw, 128)
        dst = q_buf.at[c, rows_of(me, own)]
        return move(query.at[:, pl.ds(col, qw)], dst, q_send, q_recv, c, k)

    def o_copy(c, k):
        col = pl.multiple_of(pair_index(other(k), c) * ow, 128)
        dst = o_buf.at[c, rows_of(me, own)]
        return move(d_attn.at[:, pl.ds(col, ow)], dst, o_send, o_recv, c, k)

    def dq_copy(c, k):
        col = pl.multiple_of(pair_index(me, c) * qw, 128)
        src = dq_buf.at[c, rows_of(other(k), own)]
        return move(src, d_query.at[:, pl.ds(col, qw)], dq_send, dq_recv, c, k)

    def w_columns(c):
        return pl.ds(pl.multiple_of(lax.rem(c, pairs) * cw, cw), cw)

    def w_own(c):
        dst = w_buf.at[c, rows_of(dp, depth)]
        return pltpu.make_async_copy(w_kv.at[:, w_columns(c)], dst, px_send.at[c])

    def w_cross(c):
        dst = w_buf.at[c, rows_of(dp, depth)]
        device = across(parts - c // pairs)
        return remote(w_kv.at[:, w_columns(c)], dst, px_send.at[c], px_recv.at[c], device)

    def w_copy(c, k):
        block = w_buf.at[c, rows_of(dp, depth)]
        return remote(block, block, w_send.at[c, k], w_recv.at[c, k], beside(k))

    def dw_copy(c, k):
        src = dw_part.at[c, rows_of(lax.rem(dp + k, groups), depth)]
        return remote(src, dw_got.at[c, k], dw_send.at[c, k], dw_recv.at[c, k], beside(k))

    def dz_copy(c):
        device = across(c // pairs)
        return remote(dw_mid.at[c], dw_fin.at[c], dz_send.at[c], dz_recv.at[c], device)

    twin = me + 1 - 2 * lax.rem(me, 2)
    facing = lax.rem(me + 2, members)
    to_twin = (dp, part * members + twin)
    to_facing = (dp, part * members + facing)

    def lat_copy(side, k):
        block = lat_buf.at[side, rows_of(me, own)]
        if k == 0:
            return pltpu.make_async_copy(latent, block, lat_send.at[side, 0])
        src = latent if side == 1 else block
        if k == 3:
            src = block = lat_buf.at[side, rows_of(facing, own)]
        device = to_facing if k == 2 else to_twin
        return remote(src, block, lat_send.at[side, k], lat_recv.at[side, k], device)

    def lat_cross():
        dst = lat_buf.at[0, rows_of(me, own)]
        return remote(latent, dst, one_send.at[0], one_recv.at[0], across(1))

    def dl_copy(k):
        if k == 2:
            src, device = dl_sum, to_facing
        else:
            src, device = dl_part.at[lax.rem(twin + 2 * k, members)], to_twin
        return remote(src, dl_got.at[k], dl_send.at[k], dl_recv.at[k], device)

    def dl_cross():
        return remote(dl_mid, dl_fin, one_send.at[1], one_recv.at[1], across(parts - 1))

    def launch(c):
        for k in list(range(1, members)) + [0]:
            q_copy(c, k).start()
            o_copy(c, k).start()

        @pl.when(c < pairs)
        def _():
            w_own(c).wait()

        @pl.when(c >= pairs)
        def _():
            w_cross(c).wait_recv()

        @pl.loop(1, groups)
        def _(k):
            w_copy(c, k).start()

    barrier = pltpu.get_barrier_semaphore()

    def greet(device):
        pl.semaphore_signal(barrier, inc=1, device_id=device, device_id_type=MESH)

    for k in range(1, members):
        greet(peer(k))
    for r in range(1, parts):
        greet(across(r))

    @pl.loop(1, groups)
    def _(k):
        greet(beside(k))

    pl.semaphore_wait(barrier, members + parts + groups - 3)

    lat_cross().start()
    for k in (2, 1, 0):
        lat_copy(1, k).start()

    @pl.loop(0, pairs)
    def _(c):
        w_own(c).start()

    launch(jnp.int32(0))
    lat_copy(1, 2).wait_recv()
    lat_copy(1, 3).start()
    lat_cross().wait_recv()
    for k in (2, 1):
        lat_copy(0, k).start()
    launch(jnp.int32(1))

    @pl.loop(pairs, chunks)
    def _(c):
        w_cross(c).start()

    lat_copy(0, 2).wait_recv()
    lat_copy(0, 3).start()

    @pl.loop(2, AHEAD)
    def _(c):
        launch(c)

    dlat_acc[...] = jnp.zeros_like(dlat_acc)
    rope_acc[...] = jnp.zeros_like(rope_acc)
    lat_copy(1, 0).wait()
    for k in (1, 3):
        lat_copy(1, k).wait_recv()
        lat_copy(0, k).wait_recv()

    half = NOPE // 2
    lane = lax.broadcasted_iota(jnp.int32, (window, NOPE), 1)
    low_lane = lane < half
    near = jnp.concatenate([lat_buf[0, pad:], lat_buf[1]], axis=0)
    lat_t[...] = jnp.transpose(near[:, :KV_RANK])
    rope = near[:, KV_RANK:].astype(f32)
    empty = jnp.zeros_like(rope)
    keys[0, :, NOPE:] = jnp.concatenate([rope, empty], axis=1).astype(bf16)
    keys[2, :, NOPE:] = jnp.concatenate([empty, rope], axis=1).astype(bf16)

    def settle(c):
        @pl.loop(1, groups)
        def _(k):
            dw_copy(c, k).wait_recv()

        total = dw_part[c, rows_of(dp, depth)].astype(f32)
        for k in range(1, groups):
            total += dw_got[c, k].astype(f32)

        @pl.when(c < pairs)
        def _():
            d_w[:, w_columns(c)] = total

        @pl.when(c >= pairs)
        def _():
            dw_mid[c] = total.astype(bf16)
            dz_copy(c).start()

    @pl.loop(0, chunks)
    def _(c):
        @pl.when(c + AHEAD < chunks)
        def _():
            launch(c + AHEAD)

        @pl.when(c >= LAG)
        def _():
            settle(c - LAG)

        @pl.loop(1, groups)
        def _(k):
            w_copy(c, k).wait_recv()

        weight = w_buf.at[c]
        split = DOC_MAX
        for side, rows in ((0, slice(0, split)), (1, slice(split, window))):
            lat = lat_buf[0, pad:, :KV_RANK] if side == 0 else lat_buf[1, :, :KV_RANK]
            kv = dot(lat, weight[...], NN)
            keys[0, rows, :NOPE] = kv[:, :NOPE].astype(bf16)
            vals[0, rows] = kv[:, NOPE : 2 * NOPE].astype(bf16)
            rolled = pltpu.roll(kv[:, 2 * NOPE : 3 * NOPE], half, 1)
            lower = low_lane[rows]
            keys[1, rows, :NOPE] = jnp.where(lower, 0.0, rolled).astype(bf16)
            keys[1, rows, NOPE:] = jnp.where(
                lower, rolled, keys[2, rows, NOPE:].astype(f32)
            ).astype(bf16)
            vals[1, rows] = kv[:, 3 * NOPE :].astype(bf16)
        for k in range(members):
            if k == 0:
                q_copy(c, k).wait()
                o_copy(c, k).wait()
            else:
                q_copy(c, k).wait_recv()
                o_copy(c, k).wait_recv()
        dk_acc[...] = jnp.zeros_like(dk_acc)
        dv_acc[...] = jnp.zeros_like(dv_acc)
        for b in range(held // QB):
            rows = slice(b * QB, (b + 1) * QB)
            span = slice(b * QB, b * QB + DOC_MAX + QB)
            shape = (DOC_MAX + QB, QB)
            key_pos = lax.broadcasted_iota(jnp.int32, shape, 0) + b * QB
            query_pos = lax.broadcasted_iota(jnp.int32, shape, 1) + (DOC_MAX + b * QB)
            allowed = (key_pos <= query_pos) & (key_pos >= starts[:, rows])
            grads = []
            for h in range(2):
                q = q_buf[c, rows, h * NOPE : h * NOPE + 2 * NOPE]
                o = o_buf[c, rows, h * VDIM : (h + 1) * VDIM]
                key = keys[h, span]
                s = dot(key, q, NT)
                s = jnp.where(allowed, s, masked_score)
                top = jnp.max(s, axis=0, keepdims=True)
                e = jnp.exp2((s - top) * to_exp2)
                probs = e * (1.0 / jnp.sum(e, axis=0, keepdims=True))
                low = probs.astype(bf16)
                dprob = dot(vals[h, span], o, NT)
                delta = jnp.sum(low.astype(f32) * dprob, axis=0, keepdims=True)
                ds = (probs * (dprob - delta)).astype(bf16)
                dv_acc[h, span] += dot(low, o, NN)
                dk_acc[h, span] += dot(ds, q, NN)
                grads.append(dot(ds, key, TN) * scale)
            a, z = grads
            dq_buf[c, rows, :NOPE] = a[:, :NOPE].astype(bf16)
            dq_buf[c, rows, NOPE : 2 * NOPE] = (a[:, NOPE:] + z[:, :NOPE]).astype(bf16)
            dq_buf[c, rows, 2 * NOPE :] = z[:, NOPE:].astype(bf16)
        for k in list(range(1, members)) + [0]:
            dq_copy(c, k).start()
        dkv[:, :NOPE] = (dk_acc[0, :, :NOPE] * scale).astype(bf16)
        dkv[:, NOPE : 2 * NOPE] = dv_acc[0].astype(bf16)
        turned_a = pltpu.roll(dk_acc[1, :, :NOPE], half, 1)
        turned_b = pltpu.roll(dk_acc[1, :, NOPE:], half, 1)
        dkv[:, 2 * NOPE : 3 * NOPE] = (jnp.where(low_lane, turned_a, turned_b) * scale).astype(bf16)
        dkv[:, 3 * NOPE :] = dv_acc[1].astype(bf16)
        dw_part[c] = dot(lat_t[...], dkv[...], NN).astype(bf16)

        @pl.loop(1, groups)
        def _(k):
            dw_copy(c, k).start()

        rope_acc[...] += dk_acc[0, :, NOPE:] + turned_b
        dlat_acc[...] += dot(dkv[...], weight[...], NT)

    for index in range(2 * members):
        side, m, first = index // members, index % members, index * own - pad
        if first < 0:
            dl_part[m, side] = jnp.zeros_like(dl_part[m, side])
        else:
            rows = slice(first, first + own)
            dl_part[m, side, :, :KV_RANK] = dlat_acc[rows].astype(bf16)
            dl_part[m, side, :, KV_RANK:] = (rope_acc[rows, :ROPE] * scale).astype(bf16)
    for k in (1, 0):
        dl_copy(k).start()
    dl_copy(1).wait_recv()
    dl_sum[...] = (dl_part[facing].astype(f32) + dl_got[1].astype(f32)).astype(bf16)
    dl_copy(2).start()

    @pl.loop(chunks - LAG, chunks)
    def _(c):
        settle(c)

    for k in (0, 2):
        dl_copy(k).wait_recv()
    back, kept = [
        dl_part[me, side].astype(f32) + dl_got[0, side].astype(f32) + dl_got[2, side].astype(f32)
        for side in range(2)
    ]
    dl_mid[...] = back.astype(bf16)
    dl_cross().start()

    @pl.loop(pairs, chunks)
    def _(c):
        dz_copy(c).wait()
        d_w[:, w_columns(c)] += dw_fin[c].astype(f32)

    dl_cross().wait()
    d_latent[...] = kept + dl_fin[...].astype(f32)

    lat_cross().wait_send()
    for k in range(1, members):
        lat_copy(0, k).wait_send()
        lat_copy(1, k).wait_send()
        dl_copy(k - 1).wait_send()

    @pl.loop(pairs, chunks)
    def _(c):
        w_cross(c).wait_send()

    @pl.loop(0, chunks)
    def _(c):
        for k in range(members):
            if k == 0:
                dq_copy(c, k).wait()
            else:
                q_copy(c, k).wait_send()
                o_copy(c, k).wait_send()
                dq_copy(c, k).wait()

        @pl.loop(1, groups)
        def _(k):
            w_copy(c, k).wait_send()
            dw_copy(c, k).wait_send()


def local(query, latent, d_attn, w_kv, doc_lengths):
    group = lax.axis_size("head")
    groups = lax.axis_size("dp")
    head = lax.axis_index("head")
    own, wide = latent.shape
    members = min(MEMBERS, group // 2)
    parts = group // members
    held = members * own
    depth = w_kv.shape[0]
    pairs = w_kv.shape[1] // (2 * (NOPE + VDIM))
    chunks = parts * pairs
    window = DOC_MAX + held
    first = (head // members) * held

    ends = jnp.cumsum(doc_lengths[0])
    positions = first + jnp.arange(held, dtype=jnp.int32)
    starts = jnp.max(jnp.where(ends[None, :] <= positions[:, None], ends[None, :], 0), axis=1)
    starts = (starts - first + DOC_MAX).astype(jnp.int32)[None, :]

    hbm = pl.BlockSpec(memory_space=pl.ANY)
    vmem = pl.BlockSpec(memory_space=pltpu.VMEM)
    bf16, f32 = jnp.bfloat16, jnp.float32
    qw, ow, cw = 2 * (NOPE + ROPE), 2 * VDIM, 2 * (NOPE + VDIM)
    by_member = pltpu.SemaphoreType.DMA((chunks, members))
    by_group = pltpu.SemaphoreType.DMA((chunks, groups))
    by_chunk = pltpu.SemaphoreType.DMA((chunks,))
    few = pltpu.SemaphoreType.DMA((2, members))
    return pl.pallas_call(
        functools.partial(kernel, (members, parts, pairs, groups)),
        out_shape=(
            jax.ShapeDtypeStruct(query.shape, bf16),
            jax.ShapeDtypeStruct(latent.shape, f32),
            jax.ShapeDtypeStruct(w_kv.shape, f32),
        ),
        in_specs=[hbm, hbm, hbm, hbm, vmem],
        out_specs=(hbm, vmem, vmem),
        scratch_shapes=[
            pltpu.VMEM((chunks, held, qw), bf16),
            pltpu.VMEM((chunks, held, ow), bf16),
            pltpu.VMEM((chunks, held, qw), bf16),
            pltpu.VMEM((chunks, KV_RANK, cw), bf16),
            pltpu.VMEM((2, held, wide), bf16),
            pltpu.VMEM((KV_RANK, window), bf16),
            pltpu.VMEM((3, window, 2 * NOPE), bf16),
            pltpu.VMEM((2, window, VDIM), bf16),
            pltpu.VMEM((2, window, 2 * NOPE), f32),
            pltpu.VMEM((2, window, VDIM), f32),
            pltpu.VMEM((window, cw), bf16),
            pltpu.VMEM((window, KV_RANK), f32),
            pltpu.VMEM((window, NOPE), f32),
            pltpu.VMEM((chunks, KV_RANK, cw), bf16),
            pltpu.VMEM((chunks, groups, depth, cw), bf16),
            pltpu.VMEM((chunks, depth, cw), bf16),
            pltpu.VMEM((chunks, depth, cw), bf16),
            pltpu.VMEM((members, 2, own, wide), bf16),
            pltpu.VMEM((2, own, wide), bf16),
            pltpu.VMEM((3, 2, own, wide), bf16),
            pltpu.VMEM((own, wide), bf16),
            pltpu.VMEM((own, wide), bf16),
        ]
        + [by_member] * 6
        + [by_group] * 2
        + [by_chunk] * 2
        + [by_group] * 2
        + [by_chunk] * 2
        + [few] * 2
        + [pltpu.SemaphoreType.DMA((members,))] * 2
        + [pltpu.SemaphoreType.DMA((2,))] * 2,
        compiler_params=pltpu.CompilerParams(
            collective_id=0, has_side_effects=True, vmem_limit_bytes=56 * 2**20
        ),
    )(query, d_attn, latent, w_kv, starts)


def solution(mesh):
    placed = (
        P(("dp", "head"), None),
        P(("dp", "head"), None),
        P(("dp", "head"), None),
        P("dp", "head"),
        P("dp", None),
    )
    return jax.shard_map(
        local,
        mesh=mesh,
        in_specs=placed,
        out_specs=(P(("dp", "head"), None), P(("dp", "head"), None), P("dp", "head")),
        check_vma=False,
    )
```
